256 devices in a mesh: sub: 64 (over z, x, core), blk: 4 (over y).
Axes of the slice: x: 4, y: 4, z: 8, core: 2. Of those that a mesh axis runs over, the one named last changes fastest.
Arguments:
- leaf_stiffness: float32 [256, 1024, 1024], P(('sub', 'blk')), may hold values from -20 to 20, as said below
- leaf_loads: float32 [256, 1024, 128], P(('sub', 'blk')), may hold values from -6 to 6
- block_maps: int32 [4, 256, 8], replicated, may hold values from 0 to 11, as said below
Outputs:
- displacements: float32 [256, 1024, 128], P(('sub', 'blk'))
The draws below stay inside these ranges and needn't reach their ends.
Inputs may be any that keep to these rules, and one draw needn't show every extreme that they name: block_maps[k, l] is the block list of the level-k node that holds leaf l, equal for all leaves of that node: 8 distinct blocks of its parent's 12; the two children of a parent together name all 12 blocks, 4 of them by both children. `leaf_stiffness`: each leaf matrix is symmetric positive definite.
All inputs are finite; a program needn't handle non-finite values.
Results may differ from the reference program's by a relative error of at most 0.0003.
Values sent between devices are 32-bit elements; how exact they have to be, the bound alone decides.
A program may use at most 192 MiB of HBM per device.

```python
import math
import jax
import jax.numpy as jnp
from jax import lax

S = 1024
BLOCK = 128
CASES = 128
LEVELS = 4
LEAVES = 256
NB = 8
IB = 4
PB = 12


def draw_leaf_stiffness(key, part):
    key = jax.random.fold_in(key, 11)
    subkeys = jax.random.split(key, 4)
    length_scale = 0.08
    low_mag = 0.5
    high_mag = 2.0
    diag_low = 0.5
    diag_high = 2.0
    points = jax.random.uniform(subkeys[0], (LEAVES, S, 3), jnp.float32)
    magnitude = jnp.exp(jax.random.uniform(subkeys[1], (LEAVES, S), jnp.float32, math.log(low_mag), math.log(high_mag)))
    sign_flip = jnp.where(jax.random.bernoulli(subkeys[2], 0.5, (LEAVES, S)), 1.0, -1.0).astype(jnp.float32)
    scaled = magnitude * sign_flip
    diag_extra = jax.random.uniform(subkeys[3], (LEAVES, S), jnp.float32, diag_low, diag_high)

    def one_leaf(entry):
        spots, factors, additions = entry
        squared = jnp.zeros((S, S), jnp.float32)
        for coord in range(3):
            differ = spots[:, None, coord] - spots[None, :, coord]
            squared = squared + differ * differ
        distance = jnp.sqrt(squared)
        kernel = factors[:, None] * factors[None, :] * jnp.exp(-distance / length_scale)
        return kernel + jnp.diag(factors * factors * additions)
    return lax.map(one_leaf, (points, scaled, diag_extra))


def draw_block_maps(key, part):
    key = jax.random.fold_in(key, 23)
    leaf_ids = jnp.arange(LEAVES, dtype=jnp.int32)
    tables = []
    for height in range(LEVELS):
        level_key = jax.random.fold_in(key, height)
        parent = leaf_ids >> height + 1
        child_side = leaf_ids >> height & 1

        def one_order(parent_id):
            return jax.random.permutation(jax.random.fold_in(level_key, parent_id), PB).astype(jnp.int32)
        orders = jax.vmap(one_order)(parent)
        first_half = orders[:, :NB]
        second_half = orders[:, IB:]
        tables.append(jnp.where(child_side[:, None] == 0, first_half, second_half).astype(jnp.int32))
    return jnp.stack(tables)


def shard_levels(key, extent, pieces, low, top_value):
    def one(axis_at, parts):
        draws = jax.random.uniform(jax.random.fold_in(jax.random.fold_in(key, 6), axis_at), (parts,), jnp.float32, low / len(pieces), top_value / len(pieces))
        return jnp.repeat(jnp.exp(draws), extent[axis_at] // parts).reshape((-1,) + (1,) * (len(extent) - axis_at - 1))

    gain = one(*pieces[0])
    for cut in pieces[1:]:
        gain = gain * one(*cut)
    return gain


def noise(rng, shape, scale, most, pieces=(), held_as=jnp.bfloat16):
    entries = scale * jax.random.normal(rng, shape, jnp.float32)
    if pieces:
        entries = entries * shard_levels(rng, shape, pieces, -0.22, 0.18)
    return jnp.clip(entries, -most, most).astype(held_as)


def setup_inputs(seed: int = 0) -> dict:
    arg_keys = jax.random.split(jax.random.key(seed), 4)
    leaf_stiffness = draw_leaf_stiffness(jax.random.fold_in(arg_keys[3], 71), 0)
    leaf_loads = noise(arg_keys[1], (LEAVES, S, CASES), 1.0, 6.0, ((0, 256),), jnp.float32)
    block_maps = draw_block_maps(jax.random.fold_in(arg_keys[3], 71), 0)
    return {"leaf_stiffness": leaf_stiffness, "leaf_loads": leaf_loads, "block_maps": block_maps}


highest = lax.Precision.HIGHEST
contract_first = (((0,), (0,)), ((), ()))

def block_table(block_list):
    parents = jnp.arange(PB, dtype=jnp.int32)
    matches = (block_list[:, None] == parents[None, :]).astype(jnp.int32)
    source = jnp.sum(matches * jnp.arange(NB, dtype=jnp.int32)[:, None], axis=0).astype(jnp.int32)
    present = jnp.sum(matches, axis=0).astype(jnp.float32)
    return (source, present)

def spread_child(stiffness, load_rows, block_list):
    source, present = block_table(block_list)
    tile_set = stiffness.reshape(NB, BLOCK, NB, BLOCK)
    tile_set = jnp.take(tile_set, source, axis=0)
    tile_set = jnp.take(tile_set, source, axis=2)
    weight = present[:, None, None, None] * present[None, None, :, None]
    matrix = (tile_set * weight).reshape(PB * BLOCK, PB * BLOCK)
    columns = load_rows.shape[-1]
    placed = jnp.take(load_rows.reshape(NB, BLOCK, columns), source, axis=0) * present[:, None, None]
    return (matrix, placed.reshape(PB * BLOCK, columns))

def interior(matrix, load_rows):
    inner_n = IB * BLOCK
    factor_low = jnp.linalg.cholesky(matrix[:inner_n, :inner_n])
    inverse_low = lax.linalg.triangular_solve(factor_low, jnp.eye(inner_n, dtype=matrix.dtype), left_side=True, lower=True)
    reduced = jnp.dot(inverse_low.astype(jnp.float32), load_rows[:inner_n].astype(jnp.float32), precision=highest, preferred_element_type=jnp.float32)
    return (inverse_low, reduced)

def coupling(matrix, inverse_low):
    inner_n = IB * BLOCK
    return jnp.dot(inverse_low.astype(jnp.float32), matrix[:inner_n, inner_n:].astype(jnp.float32), precision=highest, preferred_element_type=jnp.float32)

def schur_rows(matrix, load_rows, coupled, reduced, row_start, row_count):
    inner_n = IB * BLOCK
    picked = lax.dynamic_slice_in_dim(coupled, row_start, row_count, 1)
    block_k = lax.dynamic_slice_in_dim(matrix[inner_n:, inner_n:], row_start, row_count, 0)
    block_f = lax.dynamic_slice_in_dim(load_rows[inner_n:], row_start, row_count, 0)
    new_k = block_k - lax.dot_general(picked.astype(jnp.float32), coupled.astype(jnp.float32), contract_first, precision=highest, preferred_element_type=jnp.float32)
    new_f = block_f - lax.dot_general(picked.astype(jnp.float32), reduced.astype(jnp.float32), contract_first, precision=highest, preferred_element_type=jnp.float32)
    return (new_k, new_f)

def recover(inverse_low, coupled, reduced, boundary):
    rhs_inner = reduced - jnp.dot(coupled.astype(jnp.float32), boundary.astype(jnp.float32), precision=highest, preferred_element_type=jnp.float32)
    inner_disp = lax.dot_general(inverse_low.astype(jnp.float32), rhs_inner.astype(jnp.float32), contract_first, precision=highest, preferred_element_type=jnp.float32)
    return jnp.concatenate([inner_disp, boundary], axis=0)

def clamped(inverse_low, reduced):
    inner_disp = lax.dot_general(inverse_low.astype(jnp.float32), reduced.astype(jnp.float32), contract_first, precision=highest, preferred_element_type=jnp.float32)
    return jnp.concatenate([inner_disp, jnp.zeros((NB * BLOCK, reduced.shape[1]), reduced.dtype)], axis=0)

def child_part(whole_disp, block_list):
    columns = whole_disp.shape[1]
    picked = jnp.take(whole_disp.reshape(PB, BLOCK, columns), block_list, axis=0)
    return picked.reshape(NB * BLOCK, columns)

def assemble_pair(pair_stiff, pair_load, pair_lists):
    first_k, first_f = spread_child(pair_stiff[0], pair_load[0], pair_lists[0])
    second_k, second_f = spread_child(pair_stiff[1], pair_load[1], pair_lists[1])
    return (first_k + second_k, first_f + second_f)

def merge_entry(entry):
    pair_stiff, pair_load, pair_lists = entry
    matrix, placed = assemble_pair(pair_stiff, pair_load, pair_lists)
    inverse_low, reduced = interior(matrix, placed)
    coupled = coupling(matrix, inverse_low)
    new_k, new_f = schur_rows(matrix, placed, coupled, reduced, 0, S)
    return (new_k, new_f, inverse_low, coupled, reduced)

def finish_entry(entry):
    pair_stiff, pair_load, pair_lists = entry
    matrix, placed = assemble_pair(pair_stiff, pair_load, pair_lists)
    inverse_low, reduced = interior(matrix, placed)
    return clamped(inverse_low, reduced)

def recover_entry(entry):
    inverse_low, coupled, reduced, boundary = entry
    return recover(inverse_low, coupled, reduced, boundary)

def split_entry(entry):
    whole_disp, pair_lists = entry
    return jnp.stack([child_part(whole_disp, pair_lists[0]), child_part(whole_disp, pair_lists[1])])

def reference(leaf_stiffness, leaf_loads, block_maps):
    stiffness = leaf_stiffness
    load_rows = leaf_loads
    stored = []
    top_lists = None
    whole_disp = None
    for height in range(LEVELS):
        spacing = 2 ** height
        n_parents = stiffness.shape[0] // 2
        child_lists = block_maps[height, ::spacing].reshape(n_parents, 2, NB)
        pair_k = stiffness.reshape(n_parents, 2, S, S)
        pair_f = load_rows.reshape(n_parents, 2, S, CASES)
        if height < LEVELS - 1:
            stiffness, load_rows, inverse_low, coupled, reduced = lax.map(merge_entry, (pair_k, pair_f, child_lists))
            stored.append((inverse_low, coupled, reduced, child_lists))
        else:
            whole_disp = lax.map(finish_entry, (pair_k, pair_f, child_lists))
            top_lists = child_lists
    boundary = None
    for height in reversed(range(LEVELS)):
        if height < LEVELS - 1:
            inverse_low, coupled, reduced, child_lists = stored[height]
            whole_disp = lax.map(recover_entry, (inverse_low, coupled, reduced, boundary))
        else:
            child_lists = top_lists
        boundary = lax.map(split_entry, (whole_disp, child_lists)).reshape(-1, S, CASES)
    return boundary
```

```python
import functools

import jax
import jax.numpy as jnp
from jax import lax
from jax.experimental import pallas as pl
from jax.experimental.pallas import tpu as pltpu
from jax.sharding import PartitionSpec as P

BLOCK = 128
LEVELS = 4
NB = 8
IB = 4
PB = 12
INNER = IB * BLOCK
F32 = jnp.float32
BF16 = jnp.bfloat16
PLAIN = (((1,), (0,)), ((), ()))
FIRST = (((0,), (0,)), ((), ()))

ORDER = (
    [(0, 0)]
    + [(0, 1), (0, 2), (0, 3)]
    + [(1, 1), (1, 2), (1, 3), (2, 2), (2, 3), (3, 3)]
    + [(a, b) for b in range(4, NB) for a in range(b + 1)]
)
SLOT = {pair: t for t, pair in enumerate(ORDER)}
PAIRS = {pair: t for t, pair in enumerate([(x, y) for y in range(PB) for x in range(y + 1)])}
PARTS = ((0, 1), (1, 3), (4, 6), (10, 26))


def lane_splat(x, k):
    return jnp.broadcast_to(x[:, k : k + 1], (8, BLOCK))


def row_splat(x, i):
    return jnp.broadcast_to(x[i : i + 1], (8, BLOCK))


def factor_block(a):
    sub = lax.broadcasted_iota(jnp.int32, (8, BLOCK), 0)
    lane = lax.broadcasted_iota(jnp.int32, (8, BLOCK), 1)
    rows = [a[8 * i : 8 * i + 8] for i in range(16)]
    for p in range(16):
        r0 = 8 * p
        inside = (lane >= r0) & (lane < r0 + 8)
        top = rows[p]
        cols = [lane_splat(top, r0 + k) for k in range(8)]
        cell = {(i, k): row_splat(cols[k], i) for k in range(8) for i in range(k + 1)}
        get = lambda i, k: cell[min(i, k), max(i, k)]
        low = jnp.where(inside, jnp.where(lane - r0 == sub, 1.0, 0.0), top)
        full = low
        scale = None
        for j in range(8):
            d = cell[j, j]
            t = 1.0 / d
            s = lax.rsqrt(d)
            scale = s if scale is None else jnp.where(sub == j, s, scale)
            col = [get(i, j) for i in range(8)]
            every = None
            below = jnp.zeros((8, BLOCK), F32)
            for i in range(8):
                if i == j:
                    continue
                every = col[i] if every is None else jnp.where(sub == i, col[i], every)
                if i > j:
                    below = jnp.where(sub == i, col[i], below)
            low = low - below * (row_splat(low, j) * t)
            if p < 15:
                r = row_splat(full, j) * t
                full = jnp.where(sub == j, r, full - every * r)
            new = {}
            for i in range(8):
                for k in range(i, 8):
                    if i == j or k == j or k <= j or (p == 15 and i < j):
                        continue
                    new[i, k] = get(i, k) - (col[i] * col[k]) * t
            cell.update(new)
            if p < 15:
                for k in range(j + 1, 8):
                    cell[j, k] = col[k] * t
        rows[p] = low * scale
        for i in range(p + 1, 16):
            x = rows[i]
            e = [lane_splat(x, r0 + k) * row_splat(full, k) for k in range(8)]
            x = jnp.where(inside, 0.0, x)
            rows[i] = x - (((e[0] + e[1]) + (e[2] + e[3])) + ((e[4] + e[5]) + (e[6] + e[7])))
    return jnp.concatenate(rows, 0)


def halves(x):
    high = x.astype(BF16)
    return high, (x - high.astype(F32)).astype(BF16)


def dot3(ah, al, bh, bl, dims):
    d = functools.partial(lax.dot_general, dimension_numbers=dims, preferred_element_type=F32)
    return d(ah, bl) + d(al, bh) + d(ah, bh)


def dot6(a, b, dims):
    return lax.dot_general(
        a, b, dims, precision=lax.Precision.HIGHEST, preferred_element_type=F32
    )


def cut(i, n=1):
    return slice(i * BLOCK, (i + n) * BLOCK)


def sort_leaf(perm, leaf_k, leaf_f, tiles, loads):
    where_is = [perm[a] for a in range(NB)]
    for t, (a, b) in enumerate(ORDER):
        rows = pl.ds(pl.multiple_of(where_is[a] * BLOCK, BLOCK), BLOCK)
        columns = pl.ds(pl.multiple_of(where_is[b] * BLOCK, BLOCK), BLOCK)
        tiles[t] = leaf_k[rows, columns]
    for a in range(NB):
        rows = pl.ds(pl.multiple_of(where_is[a] * BLOCK, BLOCK), BLOCK)
        loads[a] = leaf_f[rows, :]


def kernel(ints, flts, leaf_k, leaf_f, out, *refs):
    refs = list(refs)
    take = lambda n: [refs.pop(0) for _ in range(n)]
    own_k, own_f = [leaf_k] + take(3), [leaf_f] + take(3)
    got_k, got_f, land = take(3), take(4), take(4)
    x_hi, x_lo, y_all = take(3), take(3), take(4)
    g_hi, g_lo = take(4), take(4)
    got_i, w, fac, u_a, u_b, v_buf = take(6)
    send_sem, recv_sem = take(2)

    SO, SS, QQ, TO, TS = 0, 48, 96, 128, 128 + 78 * LEVELS
    MO, MS, AHEAD = 0, 48, 96

    i_sub = lax.axis_index("sub")
    i_blk = lax.axis_index("blk")
    flip1 = lambda i: i + 1 - 2 * (i % 2)
    flip2 = lambda i: i + 2 - 4 * ((i // 2) % 2)
    partner = [
        (i_sub, flip1(i_blk)),
        (i_sub, flip2(i_blk)),
        (flip1(i_sub), i_blk),
        (flip2(i_sub), i_blk),
    ]

    barrier = pltpu.get_barrier_semaphore()
    for who in partner:
        pl.semaphore_signal(barrier, inc=1, device_id=who, device_id_type=pl.DeviceIdType.MESH)
    pl.semaphore_wait(barrier, LEVELS)

    def copies(k, part):
        if part == 4:
            n = NB if k < 3 else IB
            src, dst = own_f[k].at[pl.ds(0, n)], got_f[k].at[pl.ds(0, n)]
        else:
            start, n = PARTS[part]
            src = own_k[k].at[pl.ds(start, n)]
            dst = (got_k[k] if part == 3 else land[k]).at[pl.ds(start, n)]
        return pltpu.make_async_remote_copy(
            src_ref=src,
            dst_ref=dst,
            send_sem=send_sem.at[k, part],
            recv_sem=recv_sem.at[k, part],
            device_id=partner[k],
            device_id_type=pl.DeviceIdType.MESH,
        )

    def tile_of(k, x, y, other):
        return ints[(TS if other else TO) + 78 * k + PAIRS[x, y]]

    def weight(k, x, y, other):
        base = MS if other else MO
        return flts[base + 12 * k + x] * flts[base + 12 * k + y]

    def summed(k, x, y, theirs):
        mine = own_k[k][tile_of(k, x, y, False)] * weight(k, x, y, False)
        return mine + theirs[tile_of(k, x, y, True)] * weight(k, x, y, True)

    def summed_f(k, x):
        mine = own_f[k][ints[SO + 12 * k + x]] * flts[MO + 12 * k + x]
        return mine + got_f[k][ints[SS + 12 * k + x]] * flts[MS + 12 * k + x]

    for part in range(5):
        copies(0, part).start()

    colblk = lax.broadcasted_iota(jnp.int32, (BLOCK, INNER), 1) // BLOCK
    rr = lax.broadcasted_iota(jnp.int32, (BLOCK, BLOCK), 0)
    cc = lax.broadcasted_iota(jnp.int32, (BLOCK, BLOCK), 1)

    for k in range(LEVELS):
        copies(k, 0).wait_recv()
        got_i[0] = land[k][0]
        for i in range(1, IB):
            for j in range(i):
                w[cut(i), cut(j)] = jnp.zeros((BLOCK, BLOCK), F32)
        w[cut(0), cut(0)] = summed(k, 0, 0, got_i)

        def step(n, carry, k=k):
            at = pl.ds(pl.multiple_of(n * BLOCK, BLOCK), BLOCK)
            inv = jnp.where(rr >= cc, factor_block(w[at, at]), 0.0)
            fac[...] = inv

            @pl.when(n == 0)
            def _():
                copies(k, 1).wait_recv()
                copies(k, 2).wait_recv()
                got_i[1:10] = land[k][1:10]
                for i in range(IB):
                    for j in range(i, IB):
                        if j:
                            w[cut(i), cut(j)] = summed(k, i, j, got_i)

            inv = fac[...]
            row = dot6(inv, w[at, :], PLAIN)
            row = jnp.where(colblk == n, jnp.concatenate([inv] * IB, 1), row)
            w[at, :] = row

            @pl.when(n < IB - 1)
            def _():
                upper = jnp.where(colblk > n, row, 0.0)
                change = dot6(upper, row, FIRST)
                for i in range(1, IB):
                    old = jnp.where((colblk == n) & (n < i), 0.0, w[cut(i), :])
                    w[cut(i), :] = old - change[cut(i)]

            return carry

        lax.fori_loop(0, IB, step, 0)
        for i in range(IB):
            for j in range(IB):
                if j <= i:
                    h, l = halves(w[cut(i), cut(j)])
                else:
                    h = l = jnp.zeros((BLOCK, BLOCK), BF16)
                g_hi[k][cut(i), cut(j)] = h
                g_lo[k][cut(i), cut(j)] = l

        if k < 3:
            copies(k, 3).wait_recv()
            got_k[k][0:10] = land[k][0:10]
        copies(k, 4).wait_recv()

        def reduced(columns, k=k):
            highs, lows = [], []
            for i in range(IB):
                cells = [
                    summed_f(k, i) if a == NB else summed(k, i, IB + a, got_k[k]) for a in columns
                ]
                h, l = halves(jnp.concatenate(cells, 1))
                highs.append(h)
                lows.append(l)
            result = []
            for i in range(IB):
                depth = slice(0, (i + 1) * BLOCK)
                bh, bl = jnp.concatenate(highs[: i + 1], 0), jnp.concatenate(lows[: i + 1], 0)
                result.append(
                    dot3(g_hi[k][cut(i), depth], g_lo[k][cut(i), depth], bh, bl, PLAIN)
                )
            return result

        if k == 3:
            for i, r in enumerate(reduced([NB])):
                y_all[k][cut(i), :] = r
            break

        def keep(first, parts, k=k):
            for i, r in enumerate(parts):
                h, l = halves(r)
                x_hi[k][cut(i), first * BLOCK : first * BLOCK + r.shape[1]] = h
                x_lo[k][cut(i), first * BLOCK : first * BLOCK + r.shape[1]] = l

        def schur(a, first, last, k=k):
            change = dot3(
                x_hi[k][:, cut(a)],
                x_lo[k][:, cut(a)],
                x_hi[k][:, cut(first, last - first)],
                x_lo[k][:, cut(first, last - first)],
                FIRST,
            )
            for b in range(first, last):
                minus = change[:, cut(b - first)]
                if b == NB:
                    own_f[k + 1][a] = summed_f(k, IB + a) - minus
                    continue
                block = summed(k, IB + a, IB + b, got_k[k])
                if a != b:
                    ahead = flts[AHEAD + 78 * k + PAIRS[IB + a, IB + b]]
                    block = ahead * block + (1.0 - ahead) * block.T
                own_k[k + 1][SLOT[a, b]] = block - minus

        keep(0, reduced([0, 1, 2, 3]))
        schur(0, 0, 4)
        copies(k + 1, 0).start()
        copies(k + 1, 1).start()
        for a in range(1, 4):
            schur(a, a, 4)
        copies(k + 1, 2).start()
        rest = reduced([4, 5, 6, 7, NB])
        keep(4, rest)
        for i, r in enumerate(rest):
            y_all[k][cut(i), :] = r[:, cut(4)]
        if k < 2:
            for a in range(NB):
                schur(a, max(a, 4), NB + 1)
            copies(k + 1, 3).start()
        else:
            for a in range(IB):
                schur(a, NB, NB + 1)
        copies(k + 1, 4).start()

    def inner(k, rhs):
        h, l = halves(rhs)
        return dot3(g_hi[k][...], g_lo[k][...], h, l, FIRST)

    top = inner(3, y_all[3][...])
    now, later = u_a, u_b
    for i in range(IB):
        now[i] = top[cut(i)]
    for i in range(IB, PB):
        now[i] = jnp.zeros((BLOCK, BLOCK), F32)
    for k in reversed(range(LEVELS - 1)):
        for a in range(NB):
            block = now[ints[QQ + 8 * (k + 1) + a]]
            v_buf[cut(a), :] = block
            later[IB + a] = block
        h, l = halves(v_buf[...])
        full = slice(0, NB * BLOCK)
        rhs = y_all[k][...] - dot3(x_hi[k][:, full], x_lo[k][:, full], h, l, PLAIN)
        result = inner(k, rhs)
        for i in range(IB):
            later[i] = result[cut(i)]
        now, later = later, now
    for a in range(NB):
        out[cut(a), :] = now[ints[QQ + a]]

    for k in range(LEVELS):
        for part in range(5):
            if k == 3 and part == 3:
                continue
            copies(k, part).wait_send()


def tables(block_maps, leaf_id):
    own = block_maps[:, leaf_id]
    other = jnp.stack([block_maps[k, leaf_id ^ (1 << k)] for k in range(LEVELS)])
    blocks = jnp.arange(PB, dtype=jnp.int32)
    eight = jnp.arange(NB, dtype=jnp.int32)
    count = lambda x, axis: jnp.sum(x.astype(jnp.int32), axis)
    rank = count(own[:, None, :] < own[:, :, None], 2)
    place = (rank[:, :, None] == eight).astype(jnp.int32)
    perm = jnp.sum(place * eight[None, :, None], 1)
    sorted_own = jnp.sum(place * own[:, :, None], 1)
    boundary = jnp.concatenate([perm[1:], eight[None]], 0) + IB
    first = jnp.broadcast_to(blocks[None, :IB], (LEVELS, IB))
    order = jnp.concatenate([first, boundary], 1)

    def lookup(lists):
        source = jnp.minimum(count(lists[:, None, :] < order[:, :, None], 2), NB - 1)
        return source, count(lists[:, None, :] == order[:, :, None], 2)

    so, mo = lookup(own)
    ss, ms = lookup(other)
    up_rank = jnp.concatenate([rank[1:], eight[None]], 0) + IB
    spot = jnp.concatenate([first, up_rank], 1)
    wanted = jnp.concatenate([own[:1], sorted_own[1:]], 0)
    down = jnp.sum((wanted[:, :, None] == blocks) * spot[:, None, :], 2)
    upper_x = jnp.array([x for x, _ in PAIRS], jnp.int32)
    upper_y = jnp.array([y for _, y in PAIRS], jnp.int32)
    pick_x = (upper_x[:, None] == blocks).astype(jnp.int32)
    pick_y = (upper_y[:, None] == blocks).astype(jnp.int32)
    pick = lambda table, which: jnp.sum(table[:, None, :] * which, 2)

    def slots(source):
        p, q = pick(source, pick_x), pick(source, pick_y)
        lo, hi = jnp.minimum(p, q), jnp.maximum(p, q)
        inner = lo * IB - (lo * (lo - 1)) // 2 + hi - lo
        return jnp.where(hi < IB, inner, (hi * (hi + 1)) // 2 + lo)

    ahead = pick(order, pick_x) <= pick(order, pick_y)
    ints = [so, ss, down, slots(so), slots(ss)]
    flts = [mo, ms, ahead]
    flat = lambda parts, kind: jnp.concatenate([x.ravel().astype(kind) for x in parts])
    return flat(ints, jnp.int32), flat(flts, F32), perm[0]


def shards(leaf_stiffness, leaf_loads, block_maps):
    leaf_id = lax.axis_index("sub") * lax.axis_size("blk") + lax.axis_index("blk")
    ints, flts, perm = tables(block_maps, leaf_id)
    vm = pltpu.VMEM
    tiles = lambda n: vm((n, BLOCK, BLOCK), F32)
    scratch = (
        [tiles(36)] * 2
        + [tiles(10)]
        + [tiles(NB)] * 3
        + [tiles(36)] * 3
        + [tiles(NB)] * 4
        + [tiles(10)] * 4
        + [vm((INNER, 9 * BLOCK), BF16)] * 6
        + [vm((INNER, BLOCK), F32)] * 4
        + [vm((INNER, INNER), BF16)] * 8
        + [tiles(10), vm((INNER, INNER), F32), vm((BLOCK, BLOCK), F32)]
        + [tiles(PB)] * 2
        + [vm((NB * BLOCK, BLOCK), F32)]
        + [pltpu.SemaphoreType.DMA((LEVELS, 5)), pltpu.SemaphoreType.DMA((LEVELS, 5))]
    )
    sorted_k, sorted_f = pl.pallas_call(
        sort_leaf,
        out_shape=[
            jax.ShapeDtypeStruct((36, BLOCK, BLOCK), F32),
            jax.ShapeDtypeStruct((NB, BLOCK, BLOCK), F32),
        ],
        in_specs=[pl.BlockSpec(memory_space=pltpu.SMEM)]
        + [pl.BlockSpec(memory_space=pltpu.VMEM)] * 2,
        out_specs=[pl.BlockSpec(memory_space=pltpu.VMEM)] * 2,
        compiler_params=pltpu.CompilerParams(vmem_limit_bytes=32 * 1024 * 1024),
    )(perm, leaf_stiffness[0], leaf_loads[0])
    out = pl.pallas_call(
        kernel,
        out_shape=jax.ShapeDtypeStruct((NB * BLOCK, BLOCK), F32),
        in_specs=[pl.BlockSpec(memory_space=pltpu.SMEM)] * 2
        + [pl.BlockSpec(memory_space=pltpu.VMEM)] * 2,
        out_specs=pl.BlockSpec(memory_space=pltpu.VMEM),
        scratch_shapes=scratch,
        compiler_params=pltpu.CompilerParams(
            collective_id=0, has_side_effects=True, vmem_limit_bytes=60 * 1024 * 1024
        ),
    )(ints, flts, sorted_k, sorted_f)
    return out[None]


def solution(mesh):
    return jax.shard_map(
        shards,
        mesh=mesh,
        in_specs=(P(("sub", "blk"), None, None), P(("sub", "blk"), None, None), P()),
        out_specs=P(("sub", "blk"), None, None),
        check_vma=False,
    )
```

```python
import functools

import jax
import jax.numpy as jnp
from jax import lax
from jax.experimental import pallas as pl
from jax.experimental.pallas import tpu as pltpu
from jax.sharding import PartitionSpec as P

BLOCK = 128
LEVELS = 4
NB = 8
IB = 4
PB = 12
INNER = IB * BLOCK
F32 = jnp.float32
BF16 = jnp.bfloat16
PLAIN = (((1,), (0,)), ((), ()))
FIRST = (((0,), (0,)), ((), ()))

ORDER = (
    [(0, 0)]
    + [(0, 1), (0, 2), (0, 3)]
    + [(1, 1), (1, 2), (1, 3), (2, 2), (2, 3), (3, 3)]
    + [(a, b) for b in range(4, NB) for a in range(b + 1)]
)
SLOT = {pair: t for t, pair in enumerate(ORDER)}
PAIRS = {pair: t for t, pair in enumerate([(x, y) for y in range(PB) for x in range(y + 1)])}
PARTS = ((0, 1), (1, 9), (10, 13), (23, 13))
LOADS = 4
HALF = BLOCK // 2


def lane_splat(x, k):
    return jnp.broadcast_to(x[:, k : k + 1], (8, BLOCK))


def row_splat(x, i):
    return jnp.broadcast_to(x[i : i + 1], (8, BLOCK))


def factor_block(a):
    sub = lax.broadcasted_iota(jnp.int32, (8, BLOCK), 0)
    lane = lax.broadcasted_iota(jnp.int32, (8, BLOCK), 1)
    rows = [a[8 * i : 8 * i + 8] for i in range(16)]
    for p in range(16):
        r0 = 8 * p
        inside = (lane >= r0) & (lane < r0 + 8)
        top = rows[p]
        cols = [lane_splat(top, r0 + k) for k in range(8)]
        cell = {(i, k): row_splat(cols[k], i) for k in range(8) for i in range(k + 1)}
        get = lambda i, k: cell[min(i, k), max(i, k)]
        low = jnp.where(inside, jnp.where(lane - r0 == sub, 1.0, 0.0), top)
        full = low
        scale = None
        for j in range(8):
            d = cell[j, j]
            t = 1.0 / d
            s = lax.rsqrt(d)
            scale = s if scale is None else jnp.where(sub == j, s, scale)
            col = [get(i, j) for i in range(8)]
            every = None
            below = jnp.zeros((8, BLOCK), F32)
            for i in range(8):
                if i == j:
                    continue
                every = col[i] if every is None else jnp.where(sub == i, col[i], every)
                if i > j:
                    below = jnp.where(sub == i, col[i], below)
            low = low - below * (row_splat(low, j) * t)
            if p < 15:
                r = row_splat(full, j) * t
                full = jnp.where(sub == j, r, full - every * r)
            new = {}
            for i in range(8):
                for k in range(i, 8):
                    if i == j or k == j or k <= j or (p == 15 and i < j):
                        continue
                    new[i, k] = get(i, k) - (col[i] * col[k]) * t
            cell.update(new)
            if p < 15:
                for k in range(j + 1, 8):
                    cell[j, k] = col[k] * t
        rows[p] = low * scale
        for i in range(p + 1, 16):
            x = rows[i]
            e = [lane_splat(x, r0 + k) * row_splat(full, k) for k in range(8)]
            x = jnp.where(inside, 0.0, x)
            rows[i] = x - (((e[0] + e[1]) + (e[2] + e[3])) + ((e[4] + e[5]) + (e[6] + e[7])))
    return jnp.concatenate(rows, 0)


def halves(x):
    high = x.astype(BF16)
    return high, (x - high.astype(F32)).astype(BF16)


def dot3(ah, al, bh, bl, dims):
    d = functools.partial(lax.dot_general, dimension_numbers=dims, preferred_element_type=F32)
    return d(ah, bl) + d(al, bh) + d(ah, bh)


def dot6(a, b, dims):
    return lax.dot_general(
        a, b, dims, precision=lax.Precision.HIGHEST, preferred_element_type=F32
    )


def cut(i, n=1):
    return slice(i * BLOCK, (i + n) * BLOCK)


def sort_leaf(listed, leaf_k, leaf_f, tiles, loads):
    place = [listed[o] for o in range(NB)]
    rank = [sum(jnp.where(q < p, 1, 0) for q in place) for p in place]
    perm = [sum(jnp.where(rank[o] == a, o, 0) for o in range(NB)) for a in range(NB)]
    at = [pl.ds(pl.multiple_of(o * BLOCK, BLOCK), BLOCK) for o in perm]
    for t, (a, b) in enumerate(ORDER):
        tiles[t] = leaf_k[at[a], at[b]]
    for a in range(NB):
        loads[a] = leaf_f[at[a], :]


def kernel(ints, flts, leaf_k, leaf_f, out, *refs):
    refs = list(refs)
    take = lambda n: [refs.pop(0) for _ in range(n)]
    own_k, own_f = take(4), take(4)
    got_k, got_f, land = take(3), take(4), take(4)
    x_hi, x_lo, y_all = take(3), take(3), take(4)
    g_hi, g_lo = take(4), take(4)
    got_i, own_i, w, fac, u_a, u_b, v_buf = take(7)
    fill_send, fill_recv, fill_here, twin_send, twin_recv, far_send, far_recv = take(7)

    SO, SS, QQ, TO, TS = 0, 48, 96, 128, 128 + 78 * LEVELS
    MO, MS, AHEAD = 0, 48, 96

    i_sub = lax.axis_index("sub")
    i_blk = lax.axis_index("blk")
    core = i_sub % 2
    high = i_blk // 2
    flip1 = lambda i: i + 1 - 2 * (i % 2)
    flip2 = lambda i: i + 2 - 4 * ((i // 2) % 2)
    twin = (flip1(i_sub), i_blk)
    trade = (flip1(i_sub), flip1(i_blk))
    over2 = (i_sub, flip2(i_blk))
    beside = (i_sub, flip1(i_blk))
    around = (i_sub, 3 - i_blk)
    across = (flip2(i_sub), i_blk)
    moved = core != i_blk % 2

    barrier = pltpu.get_barrier_semaphore()
    friends = [twin, trade, over2, beside, around, across]
    for who in friends:
        pl.semaphore_signal(barrier, inc=1, device_id=who, device_id_type=pl.DeviceIdType.MESH)
    pl.semaphore_wait(barrier, len(friends))

    def remote(src, dst, send, recv, who):
        return pltpu.make_async_remote_copy(
            src_ref=src,
            dst_ref=dst,
            send_sem=send,
            recv_sem=recv,
            device_id=who,
            device_id_type=pl.DeviceIdType.MESH,
        )

    def span(part, k):
        return (0, NB if k < 3 else IB) if part == LOADS else PARTS[part]

    def home(k, part):
        return own_f[k] if part == LOADS else own_k[k]

    def away(k, part):
        return got_f[k] if part == LOADS else land[k] if part < 2 else got_k[k]

    def fill(part):
        start, n = span(part, 0)
        src = (leaf_f if part == LOADS else leaf_k).at[pl.ds(start, n)]
        dst = home(0, part).at[pl.ds(start, n)]
        return (
            remote(src, dst, fill_send.at[part], fill_recv.at[part], trade),
            pltpu.make_async_copy(src, dst, fill_here.at[part]),
        )

    def fill_start(part):
        there, here = fill(part)
        pl.when(moved)(there.start)
        pl.when(jnp.logical_not(moved))(here.start)

    def fill_wait(part):
        there, here = fill(part)
        pl.when(moved)(there.wait_recv)
        pl.when(jnp.logical_not(moved))(here.wait)

    def share(k, part):
        start, n = span(part, k)
        dst = away(k, part).at[pl.ds(start, n)]
        src = home(k, part).at[pl.ds(start, n)]
        if k:
            rows = pl.ds(pl.multiple_of(core * HALF, HALF), HALF)
            dst = src = away(k, part).at[pl.ds(start, n), rows, :]
        return remote(src, dst, twin_send.at[k, part], twin_recv.at[k, part], twin)

    def send(k, part):
        start, n = span(part, k)
        src, dst = home(k, part), away(k, part)
        if part == 0 or k != 2:
            who = (None, over2, beside, across)[k]
            if part == 0:
                src, dst = src.at[pl.ds(start, n)], dst.at[pl.ds(start, n)]
            else:
                rows = pl.ds(pl.multiple_of(core * HALF, HALF), HALF)
                src, dst = src.at[pl.ds(start, n), rows, :], dst.at[pl.ds(start, n), rows, :]
            return [remote(src, dst, far_send.at[k, 0, part], far_recv.at[k, 0, part], who)]
        quarter = HALF // 2
        rows = lambda q: pl.ds(pl.multiple_of(core * HALF + q * quarter, quarter), quarter)
        src = src.at[pl.ds(start, n), rows(high), :]
        dst = dst.at[pl.ds(start, n), rows(high), :]
        return [
            remote(src, dst, far_send.at[k, d, part], far_recv.at[k, high, part], who)
            for d, who in enumerate((beside, around))
        ]

    def send_start(k, part):
        for c in send(k, part):
            c.start()

    def far_wait(k, part):
        if part == 0 or k != 2:
            send(k, part)[0].wait_recv()
            return
        start, n = span(part, k)
        quarter = HALF // 2
        for q in range(2):
            rows = pl.ds(pl.multiple_of(core * HALF + q * quarter, quarter), quarter)
            ref = away(k, part).at[pl.ds(start, n), rows, :]
            remote(ref, ref, far_send.at[k, 0, part], far_recv.at[k, q, part], beside).wait_recv()

    def arrive(k, part):
        if k == 0:
            fill_wait(part)
        else:
            far_wait(k, part)
        if k == 0 or part:
            share(k, part).start()

    def complete(k, part):
        if k == 0 or part:
            share(k, part).wait_recv()

    def tile_of(k, x, y, other):
        return ints[(TS if other else TO) + 78 * k + PAIRS[x, y]]

    def weight(k, x, y, other):
        base = MS if other else MO
        return flts[base + 12 * k + x] * flts[base + 12 * k + y]

    def summed(k, x, y, ours, theirs):
        mine = ours[tile_of(k, x, y, False)] * weight(k, x, y, False)
        return mine + theirs[tile_of(k, x, y, True)] * weight(k, x, y, True)

    def summed_f(k, x):
        mine = own_f[k][ints[SO + 12 * k + x]] * flts[MO + 12 * k + x]
        return mine + got_f[k][ints[SS + 12 * k + x]] * flts[MS + 12 * k + x]

    for part in range(5):
        fill_start(part)

    colblk = lax.broadcasted_iota(jnp.int32, (BLOCK, INNER), 1) // BLOCK
    rr = lax.broadcasted_iota(jnp.int32, (BLOCK, BLOCK), 0)
    cc = lax.broadcasted_iota(jnp.int32, (BLOCK, BLOCK), 1)

    for k in range(LEVELS):
        arrive(k, 0)
        complete(k, 0)
        got_i[0] = land[k][0]
        for i in range(1, IB):
            for j in range(i):
                w[cut(i), cut(j)] = jnp.zeros((BLOCK, BLOCK), F32)
        ours = own_k[k]
        if k == 0:
            own_i[0] = own_k[0][0]
            ours = own_i
        w[cut(0), cut(0)] = summed(k, 0, 0, ours, got_i)

        def step(n, carry, k=k, ours=ours):
            at = pl.ds(pl.multiple_of(n * BLOCK, BLOCK), BLOCK)
            inv = jnp.where(rr >= cc, factor_block(w[at, at]), 0.0)
            fac[...] = inv

            @pl.when(n == 0)
            def _():
                arrive(k, 1)
                complete(k, 1)
                got_i[1:10] = land[k][1:10]
                if k == 0:
                    own_i[1:10] = own_k[0][1:10]
                for i in range(IB):
                    for j in range(i, IB):
                        if j:
                            w[cut(i), cut(j)] = summed(k, i, j, ours, got_i)

            inv = fac[...]
            row = dot6(inv, w[at, :], PLAIN)
            row = jnp.where(colblk == n, jnp.concatenate([inv] * IB, 1), row)
            w[at, :] = row

            @pl.when(n < IB - 1)
            def _():
                upper = jnp.where(colblk > n, row, 0.0)
                change = dot6(upper, row, FIRST)
                for i in range(1, IB):
                    old = jnp.where((colblk == n) & (n < i), 0.0, w[cut(i), :])
                    w[cut(i), :] = old - change[cut(i)]

            return carry

        lax.fori_loop(0, IB, step, 0)
        for i in range(IB):
            for j in range(IB):
                if j <= i:
                    h, l = halves(w[cut(i), cut(j)])
                else:
                    h = l = jnp.zeros((BLOCK, BLOCK), BF16)
                g_hi[k][cut(i), cut(j)] = h
                g_lo[k][cut(i), cut(j)] = l

        if k < 3:
            arrive(k, 2)
            arrive(k, 3)
            got_k[k][0:10] = land[k][0:10]
            complete(k, 2)
            complete(k, 3)

        def reduced(columns, k=k):
            highs, lows = [], []
            for i in range(IB):
                cells = [
                    summed_f(k, i) if a == NB else summed(k, i, IB + a, own_k[k], got_k[k]) for a in columns
                ]
                h, l = halves(jnp.concatenate(cells, 1))
                highs.append(h)
                lows.append(l)
            result = []
            for i in range(IB):
                depth = slice(0, (i + 1) * BLOCK)
                bh, bl = jnp.concatenate(highs[: i + 1], 0), jnp.concatenate(lows[: i + 1], 0)
                result.append(
                    dot3(g_hi[k][cut(i), depth], g_lo[k][cut(i), depth], bh, bl, PLAIN)
                )
            return result

        if k == 3:
            arrive(k, LOADS)
            complete(k, LOADS)
            for i, r in enumerate(reduced([NB])):
                y_all[k][cut(i), :] = r
            break

        def keep(first, parts, k=k):
            for i, r in enumerate(parts):
                h, l = halves(r)
                x_hi[k][cut(i), first * BLOCK : first * BLOCK + r.shape[1]] = h
                x_lo[k][cut(i), first * BLOCK : first * BLOCK + r.shape[1]] = l

        def schur(a, first, last, k=k):
            change = dot3(
                x_hi[k][:, cut(a)],
                x_lo[k][:, cut(a)],
                x_hi[k][:, cut(first, last - first)],
                x_lo[k][:, cut(first, last - first)],
                FIRST,
            )
            for b in range(first, last):
                minus = change[:, cut(b - first)]
                if b == NB:
                    own_f[k + 1][a] = summed_f(k, IB + a) - minus
                    continue
                block = summed(k, IB + a, IB + b, own_k[k], got_k[k])
                if a != b:
                    ahead = flts[AHEAD + 78 * k + PAIRS[IB + a, IB + b]]
                    block = ahead * block + (1.0 - ahead) * block.T
                own_k[k + 1][SLOT[a, b]] = block - minus

        keep(0, reduced([0, 1, 2, 3]))
        schur(0, 0, 4)
        send_start(k + 1, 0)
        for a in range(1, 4):
            schur(a, a, 4)
        send_start(k + 1, 1)
        arrive(k, LOADS)
        complete(k, LOADS)
        rest = reduced([4, 5, 6, 7, NB])
        keep(4, rest)
        for i, r in enumerate(rest):
            y_all[k][cut(i), :] = r[:, cut(4)]
        if k < 2:
            for a in range(NB):
                schur(a, max(a, 4), NB + 1)
            send_start(k + 1, 2)
            send_start(k + 1, 3)
        else:
            for a in range(IB):
                schur(a, NB, NB + 1)
        send_start(k + 1, LOADS)

    def inner(k, rhs):
        h, l = halves(rhs)
        return dot3(g_hi[k][...], g_lo[k][...], h, l, FIRST)

    top = inner(3, y_all[3][...])
    now, later = u_a, u_b
    for i in range(IB):
        now[i] = top[cut(i)]
    for i in range(IB, PB):
        now[i] = jnp.zeros((BLOCK, BLOCK), F32)
    for k in reversed(range(LEVELS - 1)):
        for a in range(NB):
            block = now[ints[QQ + 8 * (k + 1) + a]]
            v_buf[cut(a), :] = block
            later[IB + a] = block
        h, l = halves(v_buf[...])
        full = slice(0, NB * BLOCK)
        rhs = y_all[k][...] - dot3(x_hi[k][:, full], x_lo[k][:, full], h, l, PLAIN)
        result = inner(k, rhs)
        for i in range(IB):
            later[i] = result[cut(i)]
        now, later = later, now
    for a in range(NB):
        v_buf[cut(a), :] = now[ints[QQ + a]]
    back = remote(v_buf, out, fill_send.at[5], fill_recv.at[5], trade)
    pl.when(moved)(back.start)

    @pl.when(jnp.logical_not(moved))
    def _():
        out[...] = v_buf[...]

    @pl.when(moved)
    def _():
        back.wait()
        for part in range(5):
            fill(part)[0].wait_send()

    for k in range(LEVELS):
        for part in range(5):
            if k == 3 and part in (2, 3):
                continue
            if k:
                for c in send(k, part):
                    c.wait_send()
            if k == 0 or part:
                share(k, part).wait_send()


def tables(block_maps, leaf_id):
    own = block_maps[:, leaf_id]
    other = jnp.stack([block_maps[k, leaf_id ^ (1 << k)] for k in range(LEVELS)])
    blocks = jnp.arange(PB, dtype=jnp.int32)
    eight = jnp.arange(NB, dtype=jnp.int32)
    count = lambda x, axis: jnp.sum(x.astype(jnp.int32), axis)
    rank = count(own[:, None, :] < own[:, :, None], 2)
    place = (rank[:, :, None] == eight).astype(jnp.int32)
    perm = jnp.sum(place * eight[None, :, None], 1)
    sorted_own = jnp.sum(place * own[:, :, None], 1)
    boundary = jnp.concatenate([perm[1:], eight[None]], 0) + IB
    first = jnp.broadcast_to(blocks[None, :IB], (LEVELS, IB))
    order = jnp.concatenate([first, boundary], 1)

    def lookup(lists):
        source = jnp.minimum(count(lists[:, None, :] < order[:, :, None], 2), NB - 1)
        return source, count(lists[:, None, :] == order[:, :, None], 2)

    so, mo = lookup(own)
    ss, ms = lookup(other)
    up_rank = jnp.concatenate([rank[1:], eight[None]], 0) + IB
    spot = jnp.concatenate([first, up_rank], 1)
    wanted = jnp.concatenate([own[:1], sorted_own[1:]], 0)
    down = jnp.sum((wanted[:, :, None] == blocks) * spot[:, None, :], 2)
    upper_x = jnp.array([x for x, _ in PAIRS], jnp.int32)
    upper_y = jnp.array([y for _, y in PAIRS], jnp.int32)
    pick_x = (upper_x[:, None] == blocks).astype(jnp.int32)
    pick_y = (upper_y[:, None] == blocks).astype(jnp.int32)
    pick = lambda table, which: jnp.sum(table[:, None, :] * which, 2)

    def slots(source):
        p, q = pick(source, pick_x), pick(source, pick_y)
        lo, hi = jnp.minimum(p, q), jnp.maximum(p, q)
        inner = lo * IB - (lo * (lo - 1)) // 2 + hi - lo
        return jnp.where(hi < IB, inner, (hi * (hi + 1)) // 2 + lo)

    ahead = pick(order, pick_x) <= pick(order, pick_y)
    ints = [so, ss, down, slots(so), slots(ss)]
    flts = [mo, ms, ahead]
    flat = lambda parts, kind: jnp.concatenate([x.ravel().astype(kind) for x in parts])
    return flat(ints, jnp.int32), flat(flts, F32)


def shards(leaf_stiffness, leaf_loads, block_maps):
    i_sub, i_blk = lax.axis_index("sub"), lax.axis_index("blk")
    width = lax.axis_size("blk")
    core, low = i_sub % 2, i_blk % 2
    listed = block_maps[0, i_sub * width + i_blk]
    ints, flts = tables(block_maps, (i_sub - core + low) * width + i_blk - low + core)
    vm = pltpu.VMEM
    dma = pltpu.SemaphoreType.DMA
    anywhere = pl.BlockSpec(memory_space=pl.ANY)
    inside = pl.BlockSpec(memory_space=pltpu.VMEM)
    tiles = lambda n: vm((n, BLOCK, BLOCK), F32)
    scratch = (
        [tiles(36)] * 3
        + [tiles(10)]
        + [tiles(NB)] * 4
        + [tiles(36)] * 3
        + [tiles(NB)] * 4
        + [tiles(10)] * 4
        + [vm((INNER, 9 * BLOCK), BF16)] * 6
        + [vm((INNER, BLOCK), F32)] * 4
        + [vm((INNER, INNER), BF16)] * 8
        + [tiles(10), tiles(10), vm((INNER, INNER), F32), vm((BLOCK, BLOCK), F32)]
        + [tiles(PB)] * 2
        + [vm((NB * BLOCK, BLOCK), F32)]
        + [dma((6,)), dma((6,)), dma((5,))]
        + [dma((LEVELS, 5))] * 2
        + [dma((LEVELS, 2, 5))] * 2
    )
    sorted_k, sorted_f = pl.pallas_call(
        sort_leaf,
        out_shape=[
            jax.ShapeDtypeStruct((36, BLOCK, BLOCK), F32),
            jax.ShapeDtypeStruct((NB, BLOCK, BLOCK), F32),
        ],
        in_specs=[pl.BlockSpec(memory_space=pltpu.SMEM)] + [inside] * 2,
        out_specs=[inside] * 2,
        compiler_params=pltpu.CompilerParams(vmem_limit_bytes=32 * 1024 * 1024),
    )(listed, leaf_stiffness[0], leaf_loads[0])
    out = pl.pallas_call(
        kernel,
        out_shape=jax.ShapeDtypeStruct((NB * BLOCK, BLOCK), F32),
        in_specs=[pl.BlockSpec(memory_space=pltpu.SMEM)] * 2 + [anywhere] * 2,
        out_specs=pl.BlockSpec(memory_space=pltpu.VMEM),
        scratch_shapes=scratch,
        compiler_params=pltpu.CompilerParams(
            collective_id=0, has_side_effects=True, vmem_limit_bytes=60 * 1024 * 1024
        ),
    )(ints, flts, sorted_k, sorted_f)
    return out[None]


def solution(mesh):
    return jax.shard_map(
        shards,
        mesh=mesh,
        in_specs=(P(("sub", "blk"), None, None), P(("sub", "blk"), None, None), P()),
        out_specs=P(("sub", "blk"), None, None),
        check_vma=False,
    )
```

```python
import functools

import jax
import jax.numpy as jnp
from jax import lax
from jax.experimental import pallas as pl
from jax.experimental.pallas import tpu as pltpu
from jax.sharding import PartitionSpec as P

BLOCK = 128
LEVELS = 4
NB = 8
IB = 4
PB = 12
INNER = IB * BLOCK
F32 = jnp.float32
BF16 = jnp.bfloat16
PLAIN = (((1,), (0,)), ((), ()))
FIRST = (((0,), (0,)), ((), ()))

ORDER = (
    [(0, 0)]
    + [(0, 1), (0, 2), (0, 3)]
    + [(1, 1), (1, 2), (1, 3), (2, 2), (2, 3), (3, 3)]
    + [(a, b) for b in range(4, NB) for a in range(b + 1)]
)
SLOT = {pair: t for t, pair in enumerate(ORDER)}
PAIRS = {pair: t for t, pair in enumerate([(x, y) for y in range(PB) for x in range(y + 1)])}
PARTS = ((0, 1), (1, 9), (10, 13), (23, 13))
LOADS = 4
HALF = BLOCK // 2


def lane_splat(x, k):
    return jnp.broadcast_to(x[:, k : k + 1], (8, BLOCK))


def row_splat(x, i):
    return jnp.broadcast_to(x[i : i + 1], (8, BLOCK))


def factor_block(a):
    sub = lax.broadcasted_iota(jnp.int32, (8, BLOCK), 0)
    lane = lax.broadcasted_iota(jnp.int32, (8, BLOCK), 1)
    rows = [a[8 * i : 8 * i + 8] for i in range(16)]
    for p in range(16):
        r0 = 8 * p
        inside = (lane >= r0) & (lane < r0 + 8)
        top = rows[p]
        cols = [lane_splat(top, r0 + k) for k in range(8)]
        cell = {(i, k): row_splat(cols[k], i) for k in range(8) for i in range(k + 1)}
        get = lambda i, k: cell[min(i, k), max(i, k)]
        low = jnp.where(inside, jnp.where(lane - r0 == sub, 1.0, 0.0), top)
        full = low
        scale = None
        for j in range(8):
            d = cell[j, j]
            t = 1.0 / d
            s = lax.rsqrt(d)
            scale = s if scale is None else jnp.where(sub == j, s, scale)
            col = [get(i, j) for i in range(8)]
            every = None
            below = jnp.zeros((8, BLOCK), F32)
            for i in range(8):
                if i == j:
                    continue
                every = col[i] if every is None else jnp.where(sub == i, col[i], every)
                if i > j:
                    below = jnp.where(sub == i, col[i], below)
            low = low - below * (row_splat(low, j) * t)
            if p < 15:
                r = row_splat(full, j) * t
                full = jnp.where(sub == j, r, full - every * r)
            new = {}
            for i in range(8):
                for k in range(i, 8):
                    if i == j or k == j or k <= j or (p == 15 and i < j):
                        continue
                    new[i, k] = get(i, k) - (col[i] * col[k]) * t
            cell.update(new)
            if p < 15:
                for k in range(j + 1, 8):
                    cell[j, k] = col[k] * t
        rows[p] = low * scale
        for i in range(p + 1, 16):
            x = rows[i]
            e = [lane_splat(x, r0 + k) * row_splat(full, k) for k in range(8)]
            x = jnp.where(inside, 0.0, x)
            rows[i] = x - (((e[0] + e[1]) + (e[2] + e[3])) + ((e[4] + e[5]) + (e[6] + e[7])))
    return jnp.concatenate(rows, 0)


def halves(x):
    high = x.astype(BF16)
    return high, (x - high.astype(F32)).astype(BF16)


def dot3(ah, al, bh, bl, dims):
    d = functools.partial(lax.dot_general, dimension_numbers=dims, preferred_element_type=F32)
    return d(ah, bl) + d(al, bh) + d(ah, bh)


def stacked3(a, b, axis):
    (ah, al), (bh, bl) = a, b
    return lax.dot_general(
        jnp.concatenate([ah, ah, al], axis),
        jnp.concatenate([bh, bl, bh], 0),
        (((axis,), (0,)), ((), ())),
        preferred_element_type=F32,
    )


def narrow3(ah, al, b, dims):
    bh, bl = halves(b)
    d = functools.partial(lax.dot_general, dimension_numbers=dims, preferred_element_type=F32)
    both = d(ah, jnp.concatenate([bh, bl], 1))
    return both[:, BLOCK:] + d(al, bh) + both[:, :BLOCK]


def cut(i, n=1):
    return slice(i * BLOCK, (i + n) * BLOCK)


def sort_leaf(listed, leaf_k, leaf_f, tiles, loads):
    place = [listed[o] for o in range(NB)]
    rank = [sum(jnp.where(q < p, 1, 0) for q in place) for p in place]
    perm = [sum(jnp.where(rank[o] == a, o, 0) for o in range(NB)) for a in range(NB)]
    at = [pl.ds(pl.multiple_of(o * BLOCK, BLOCK), BLOCK) for o in perm]
    for t, (a, b) in enumerate(ORDER):
        tiles[t] = leaf_k[at[a], at[b]]
    for a in range(NB):
        loads[a] = leaf_f[at[a], :]


def kernel(ints, flts, leaf_k, leaf_f, out, *refs):
    refs = list(refs)
    take = lambda n: [refs.pop(0) for _ in range(n)]
    own_k, own_f = take(4), take(4)
    got_k, got_f, land = take(3), take(4), take(4)
    x_hi, x_lo, y_all = take(3), take(3), take(4)
    g_hi, g_lo = take(4), take(4)
    got_i, own_i, w, fac, u_a, u_b, v_buf = take(7)
    fill_send, fill_recv, fill_here, twin_send, twin_recv, far_send, far_recv = take(7)

    SO, SS, QQ, TO, TS = 0, 48, 96, 128, 128 + 78 * LEVELS
    MO, MS, AHEAD = 0, 48, 96

    i_sub = lax.axis_index("sub")
    i_blk = lax.axis_index("blk")
    core = i_sub % 2
    high = i_blk // 2
    flip1 = lambda i: i + 1 - 2 * (i % 2)
    flip2 = lambda i: i + 2 - 4 * ((i // 2) % 2)
    twin = (flip1(i_sub), i_blk)
    trade = (flip1(i_sub), flip1(i_blk))
    over2 = (i_sub, flip2(i_blk))
    beside = (i_sub, flip1(i_blk))
    around = (i_sub, 3 - i_blk)
    across = (flip2(i_sub), i_blk)
    moved = core != i_blk % 2

    barrier = pltpu.get_barrier_semaphore()
    friends = [twin, trade, over2, beside, around, across]
    for who in friends:
        pl.semaphore_signal(barrier, inc=1, device_id=who, device_id_type=pl.DeviceIdType.MESH)
    pl.semaphore_wait(barrier, len(friends))

    def remote(src, dst, send, recv, who):
        return pltpu.make_async_remote_copy(
            src_ref=src,
            dst_ref=dst,
            send_sem=send,
            recv_sem=recv,
            device_id=who,
            device_id_type=pl.DeviceIdType.MESH,
        )

    def span(part, k):
        return (0, NB if k < 3 else IB) if part == LOADS else PARTS[part]

    def home(k, part):
        return own_f[k] if part == LOADS else own_k[k]

    def away(k, part):
        return got_f[k] if part == LOADS else land[k] if part < 2 else got_k[k]

    def fill(part):
        start, n = span(part, 0)
        src = (leaf_f if part == LOADS else leaf_k).at[pl.ds(start, n)]
        dst = home(0, part).at[pl.ds(start, n)]
        return (
            remote(src, dst, fill_send.at[part], fill_recv.at[part], trade),
            pltpu.make_async_copy(src, dst, fill_here.at[part]),
        )

    def fill_start(part):
        there, here = fill(part)
        pl.when(moved)(there.start)
        pl.when(jnp.logical_not(moved))(here.start)

    def fill_wait(part):
        there, here = fill(part)
        pl.when(moved)(there.wait_recv)
        pl.when(jnp.logical_not(moved))(here.wait)

    def share(k, part):
        start, n = span(part, k)
        dst = away(k, part).at[pl.ds(start, n)]
        src = home(k, part).at[pl.ds(start, n)]
        if k:
            rows = pl.ds(pl.multiple_of(core * HALF, HALF), HALF)
            dst = src = away(k, part).at[pl.ds(start, n), rows, :]
        return remote(src, dst, twin_send.at[k, part], twin_recv.at[k, part], twin)

    def send(k, part):
        start, n = span(part, k)
        src, dst = home(k, part), away(k, part)
        if part == 0 or k != 2:
            who = (None, over2, beside, across)[k]
            if part == 0:
                src, dst = src.at[pl.ds(start, n)], dst.at[pl.ds(start, n)]
            else:
                rows = pl.ds(pl.multiple_of(core * HALF, HALF), HALF)
                src, dst = src.at[pl.ds(start, n), rows, :], dst.at[pl.ds(start, n), rows, :]
            return [remote(src, dst, far_send.at[k, 0, part], far_recv.at[k, 0, part], who)]
        quarter = HALF // 2
        rows = lambda q: pl.ds(pl.multiple_of(core * HALF + q * quarter, quarter), quarter)
        src = src.at[pl.ds(start, n), rows(high), :]
        dst = dst.at[pl.ds(start, n), rows(high), :]
        return [
            remote(src, dst, far_send.at[k, d, part], far_recv.at[k, high, part], who)
            for d, who in enumerate((beside, around))
        ]

    def send_start(k, part):
        for c in send(k, part):
            c.start()

    def far_wait(k, part):
        if part == 0 or k != 2:
            send(k, part)[0].wait_recv()
            return
        start, n = span(part, k)
        quarter = HALF // 2
        for q in range(2):
            rows = pl.ds(pl.multiple_of(core * HALF + q * quarter, quarter), quarter)
            ref = away(k, part).at[pl.ds(start, n), rows, :]
            remote(ref, ref, far_send.at[k, 0, part], far_recv.at[k, q, part], beside).wait_recv()

    def arrive(k, part):
        if k == 0:
            fill_wait(part)
        else:
            far_wait(k, part)
        if k == 0 or part:
            share(k, part).start()

    def complete(k, part):
        if k == 0 or part:
            share(k, part).wait_recv()

    def tile_of(k, x, y, other):
        return ints[(TS if other else TO) + 78 * k + PAIRS[x, y]]

    def weight(k, x, y, other):
        base = MS if other else MO
        return flts[base + 12 * k + x] * flts[base + 12 * k + y]

    def summed(k, x, y, ours, theirs):
        mine = ours[tile_of(k, x, y, False)] * weight(k, x, y, False)
        return mine + theirs[tile_of(k, x, y, True)] * weight(k, x, y, True)

    def summed_f(k, x):
        mine = own_f[k][ints[SO + 12 * k + x]] * flts[MO + 12 * k + x]
        return mine + got_f[k][ints[SS + 12 * k + x]] * flts[MS + 12 * k + x]

    for part in range(5):
        fill_start(part)

    colblk = lax.broadcasted_iota(jnp.int32, (BLOCK, INNER), 1) // BLOCK
    rr = lax.broadcasted_iota(jnp.int32, (BLOCK, BLOCK), 0)
    cc = lax.broadcasted_iota(jnp.int32, (BLOCK, BLOCK), 1)

    for k in range(LEVELS):
        arrive(k, 0)
        complete(k, 0)
        got_i[0] = land[k][0]
        for i in range(1, IB):
            for j in range(i):
                w[cut(i), cut(j)] = jnp.zeros((BLOCK, BLOCK), F32)
        ours = own_k[k]
        if k == 0:
            own_i[0] = own_k[0][0]
            ours = own_i
        w[cut(0), cut(0)] = summed(k, 0, 0, ours, got_i)

        def step(n, carry, k=k, ours=ours):
            at = pl.ds(pl.multiple_of(n * BLOCK, BLOCK), BLOCK)
            inv = jnp.where(rr >= cc, factor_block(w[at, at]), 0.0)
            fac[...] = inv

            @pl.when(n == 0)
            def _():
                arrive(k, 1)
                complete(k, 1)
                got_i[1:10] = land[k][1:10]
                if k == 0:
                    own_i[1:10] = own_k[0][1:10]
                for i in range(IB):
                    for j in range(i, IB):
                        if j:
                            w[cut(i), cut(j)] = summed(k, i, j, ours, got_i)

            inv = fac[...]
            row = stacked3(halves(inv), halves(w[at, :]), 1)
            row = jnp.where(colblk == n, jnp.concatenate([inv] * IB, 1), row)
            w[at, :] = row

            @pl.when(n < IB - 1)
            def _():
                upper = jnp.where(colblk > n, row, 0.0)[:, BLOCK:]
                change = stacked3(halves(upper), halves(row), 0)
                for i in range(1, IB):
                    old = jnp.where((colblk == n) & (n < i), 0.0, w[cut(i), :])
                    w[cut(i), :] = old - change[cut(i - 1)]

            return carry

        lax.fori_loop(0, IB, step, 0)
        for i in range(IB):
            for j in range(IB):
                if j <= i:
                    h, l = halves(w[cut(i), cut(j)])
                else:
                    h = l = jnp.zeros((BLOCK, BLOCK), BF16)
                g_hi[k][cut(i), cut(j)] = h
                g_lo[k][cut(i), cut(j)] = l

        if k < 3:
            arrive(k, 2)
            arrive(k, 3)
            got_k[k][0:10] = land[k][0:10]
            complete(k, 2)
            complete(k, 3)

        def reduced(columns, k=k):
            highs, lows = [], []
            for i in range(IB):
                cells = [
                    summed_f(k, i) if a == NB else summed(k, i, IB + a, own_k[k], got_k[k]) for a in columns
                ]
                h, l = halves(jnp.concatenate(cells, 1))
                highs.append(h)
                lows.append(l)
            result = []
            for i in range(IB):
                depth = slice(0, (i + 1) * BLOCK)
                bh, bl = jnp.concatenate(highs[: i + 1], 0), jnp.concatenate(lows[: i + 1], 0)
                result.append(
                    dot3(g_hi[k][cut(i), depth], g_lo[k][cut(i), depth], bh, bl, PLAIN)
                )
            return result

        if k == 3:
            arrive(k, LOADS)
            complete(k, LOADS)
            for i, r in enumerate(reduced([NB])):
                y_all[k][cut(i), :] = r
            break

        def keep(first, parts, k=k):
            for i, r in enumerate(parts):
                h, l = halves(r)
                x_hi[k][cut(i), first * BLOCK : first * BLOCK + r.shape[1]] = h
                x_lo[k][cut(i), first * BLOCK : first * BLOCK + r.shape[1]] = l

        def schur(a, first, last, k=k):
            change = dot3(
                x_hi[k][:, cut(a)],
                x_lo[k][:, cut(a)],
                x_hi[k][:, cut(first, last - first)],
                x_lo[k][:, cut(first, last - first)],
                FIRST,
            )
            for b in range(first, last):
                minus = change[:, cut(b - first)]
                if b == NB:
                    own_f[k + 1][a] = summed_f(k, IB + a) - minus
                    continue
                block = summed(k, IB + a, IB + b, own_k[k], got_k[k])
                if a != b:
                    ahead = flts[AHEAD + 78 * k + PAIRS[IB + a, IB + b]]
                    block = ahead * block + (1.0 - ahead) * block.T
                own_k[k + 1][SLOT[a, b]] = block - minus

        keep(0, reduced([0, 1, 2, 3]))
        schur(0, 0, 4)
        send_start(k + 1, 0)
        for a in range(1, 4):
            schur(a, a, 4)
        send_start(k + 1, 1)
        arrive(k, LOADS)
        complete(k, LOADS)
        rest = reduced([4, 5, 6, 7, NB])
        keep(4, rest)
        for i, r in enumerate(rest):
            y_all[k][cut(i), :] = r[:, cut(4)]
        if k < 2:
            for a in range(NB):
                schur(a, max(a, 4), NB + 1)
            send_start(k + 1, 2)
            send_start(k + 1, 3)
        else:
            for a in range(IB):
                schur(a, NB, NB + 1)
        send_start(k + 1, LOADS)

    def inner(k, rhs):
        return narrow3(g_hi[k][...], g_lo[k][...], rhs, FIRST)

    top = inner(3, y_all[3][...])
    now, later = u_a, u_b
    for i in range(IB):
        now[i] = top[cut(i)]
    for i in range(IB, PB):
        now[i] = jnp.zeros((BLOCK, BLOCK), F32)
    for k in reversed(range(LEVELS - 1)):
        for a in range(NB):
            block = now[ints[QQ + 8 * (k + 1) + a]]
            v_buf[cut(a), :] = block
            later[IB + a] = block
        full = slice(0, NB * BLOCK)
        rhs = y_all[k][...] - narrow3(x_hi[k][:, full], x_lo[k][:, full], v_buf[...], PLAIN)
        result = inner(k, rhs)
        for i in range(IB):
            later[i] = result[cut(i)]
        now, later = later, now
    for a in range(NB):
        v_buf[cut(a), :] = now[ints[QQ + a]]
    back = remote(v_buf, out, fill_send.at[5], fill_recv.at[5], trade)
    pl.when(moved)(back.start)

    @pl.when(jnp.logical_not(moved))
    def _():
        out[...] = v_buf[...]

    @pl.when(moved)
    def _():
        back.wait()
        for part in range(5):
            fill(part)[0].wait_send()

    for k in range(LEVELS):
        for part in range(5):
            if k == 3 and part in (2, 3):
                continue
            if k:
                for c in send(k, part):
                    c.wait_send()
            if k == 0 or part:
                share(k, part).wait_send()


def tables(block_maps, leaf_id):
    own = block_maps[:, leaf_id]
    other = jnp.stack([block_maps[k, leaf_id ^ (1 << k)] for k in range(LEVELS)])
    blocks = jnp.arange(PB, dtype=jnp.int32)
    eight = jnp.arange(NB, dtype=jnp.int32)
    count = lambda x, axis: jnp.sum(x.astype(jnp.int32), axis)
    rank = count(own[:, None, :] < own[:, :, None], 2)
    place = (rank[:, :, None] == eight).astype(jnp.int32)
    perm = jnp.sum(place * eight[None, :, None], 1)
    sorted_own = jnp.sum(place * own[:, :, None], 1)
    boundary = jnp.concatenate([perm[1:], eight[None]], 0) + IB
    first = jnp.broadcast_to(blocks[None, :IB], (LEVELS, IB))
    order = jnp.concatenate([first, boundary], 1)

    def lookup(lists):
        source = jnp.minimum(count(lists[:, None, :] < order[:, :, None], 2), NB - 1)
        return source, count(lists[:, None, :] == order[:, :, None], 2)

    so, mo = lookup(own)
    ss, ms = lookup(other)
    up_rank = jnp.concatenate([rank[1:], eight[None]], 0) + IB
    spot = jnp.concatenate([first, up_rank], 1)
    wanted = jnp.concatenate([own[:1], sorted_own[1:]], 0)
    down = jnp.sum((wanted[:, :, None] == blocks) * spot[:, None, :], 2)
    upper_x = jnp.array([x for x, _ in PAIRS], jnp.int32)
    upper_y = jnp.array([y for _, y in PAIRS], jnp.int32)
    pick_x = (upper_x[:, None] == blocks).astype(jnp.int32)
    pick_y = (upper_y[:, None] == blocks).astype(jnp.int32)
    pick = lambda table, which: jnp.sum(table[:, None, :] * which, 2)

    def slots(source):
        p, q = pick(source, pick_x), pick(source, pick_y)
        lo, hi = jnp.minimum(p, q), jnp.maximum(p, q)
        inner = lo * IB - (lo * (lo - 1)) // 2 + hi - lo
        return jnp.where(hi < IB, inner, (hi * (hi + 1)) // 2 + lo)

    ahead = pick(order, pick_x) <= pick(order, pick_y)
    ints = [so, ss, down, slots(so), slots(ss)]
    flts = [mo, ms, ahead]
    flat = lambda parts, kind: jnp.concatenate([x.ravel().astype(kind) for x in parts])
    return flat(ints, jnp.int32), flat(flts, F32)


def shards(leaf_stiffness, leaf_loads, block_maps):
    i_sub, i_blk = lax.axis_index("sub"), lax.axis_index("blk")
    width = lax.axis_size("blk")
    core, low = i_sub % 2, i_blk % 2
    listed = block_maps[0, i_sub * width + i_blk]
    ints, flts = tables(block_maps, (i_sub - core + low) * width + i_blk - low + core)
    vm = pltpu.VMEM
    dma = pltpu.SemaphoreType.DMA
    anywhere = pl.BlockSpec(memory_space=pl.ANY)
    inside = pl.BlockSpec(memory_space=pltpu.VMEM)
    tiles = lambda n: vm((n, BLOCK, BLOCK), F32)
    scratch = (
        [tiles(36)] * 3
        + [tiles(10)]
        + [tiles(NB)] * 4
        + [tiles(36)] * 3
        + [tiles(NB)] * 4
        + [tiles(10)] * 4
        + [vm((INNER, 9 * BLOCK), BF16)] * 6
        + [vm((INNER, BLOCK), F32)] * 4
        + [vm((INNER, INNER), BF16)] * 8
        + [tiles(10), tiles(10), vm((INNER, INNER), F32), vm((BLOCK, BLOCK), F32)]
        + [tiles(PB)] * 2
        + [vm((NB * BLOCK, BLOCK), F32)]
        + [dma((6,)), dma((6,)), dma((5,))]
        + [dma((LEVELS, 5))] * 2
        + [dma((LEVELS, 2, 5))] * 2
    )
    sorted_k, sorted_f = pl.pallas_call(
        sort_leaf,
        out_shape=[
            jax.ShapeDtypeStruct((36, BLOCK, BLOCK), F32),
            jax.ShapeDtypeStruct((NB, BLOCK, BLOCK), F32),
        ],
        in_specs=[pl.BlockSpec(memory_space=pltpu.SMEM)] + [inside] * 2,
        out_specs=[inside] * 2,
        compiler_params=pltpu.CompilerParams(vmem_limit_bytes=32 * 1024 * 1024),
    )(listed, leaf_stiffness[0], leaf_loads[0])
    out = pl.pallas_call(
        kernel,
        out_shape=jax.ShapeDtypeStruct((NB * BLOCK, BLOCK), F32),
        in_specs=[pl.BlockSpec(memory_space=pltpu.SMEM)] * 2 + [anywhere] * 2,
        out_specs=pl.BlockSpec(memory_space=pltpu.VMEM),
        scratch_shapes=scratch,
        compiler_params=pltpu.CompilerParams(
            collective_id=0, has_side_effects=True, vmem_limit_bytes=60 * 1024 * 1024
        ),
    )(ints, flts, sorted_k, sorted_f)
    return out[None]


def solution(mesh):
    return jax.shard_map(
        shards,
        mesh=mesh,
        in_specs=(P(("sub", "blk"), None, None), P(("sub", "blk"), None, None), P()),
        out_specs=P(("sub", "blk"), None, None),
        check_vma=False,
    )
```
